512 devices in a mesh: row: 32 (over z, x), col: 16 (over y, core).
Axes of the slice: x: 4, y: 8, z: 8, core: 2. Of those that a mesh axis runs over, the one named last changes fastest.
Arguments:
- inputs: bfloat16 [768, 12288], P('row', 'col'), may hold values from -6 to 6
- weight: bfloat16 [12288, 49152], P('col', 'row'), may hold values from -0.0546875 to 0.0546875
- cotangent: bfloat16 [768, 49152], P('col', 'row'), may hold values from -6 to 6
Outputs:
- activated: bfloat16 [768, 49152], P('col', 'row')
- grad_inputs: bfloat16 [768, 12288], P('row', 'col')
- grad_weight: bfloat16 [12288, 49152], P('col', 'row')
The draws below stay inside these ranges and needn't reach their ends.
All inputs are finite; a program needn't handle non-finite values.
Results may differ from the reference program's by a relative error of at most 0.025.
Values may be sent and summed in bfloat16 or wider, within the bound.
No kernel may reach another device: no remote copies, remote signals or barrier semaphores. Data moves between devices by JAX's collectives and lax.ppermute only.
A program may use at most 64 MiB of HBM per device.

```python
import jax
import jax.numpy as jnp
from jax import lax

D = 12288
F = 49152
TOKENS = 768
N_ROW = 32
N_COL = 16


def levels(stream_key, dims, shards, smallest, largest):
    gain = 1.0
    for position, parts in shards:
        heights = jax.random.uniform(jax.random.fold_in(jax.random.fold_in(stream_key, 6), position), (parts,), jnp.float32, smallest / len(shards), largest / len(shards))
        gain = gain * jnp.repeat(jnp.exp(heights), dims[position] // parts).reshape((-1,) + (1,) * (len(dims) - 1 - position))
    return gain


def scatter_about(stream_key, dims, scale, reach, cuts=(), held_as=jnp.bfloat16):
    entries = jax.random.normal(stream_key, dims, jnp.float32) * scale
    if len(cuts) > 0:
        entries = levels(stream_key, dims, cuts, -0.22, 0.18) * entries
    return jnp.clip(entries, min=-reach, max=reach).astype(held_as)


def setup_inputs(seed: int = 0) -> dict:
    key_list = jax.random.split(jax.random.key(seed), 4)
    inputs = scatter_about(key_list[0], (TOKENS, D), 1.0, 6.0, ((0, 32), (1, 16)))
    weight = scatter_about(key_list[1], (D, F), D ** -0.5, 0.0546875, ((0, 16), (1, 32)))
    cotangent = scatter_about(key_list[2], (TOKENS, F), 1.0, 6.0, ((0, 16), (1, 32)))
    return dict(inputs=inputs, weight=weight, cotangent=cotangent)


def gelu_parts(preact):
    tanh_arg = 0.7978845608 * (preact + 0.044715 * preact * preact * preact)
    tanh_value = jnp.tanh(tanh_arg)
    activated = 0.5 * preact * (1.0 + tanh_value)
    slopes = 0.5 * (1.0 + tanh_value) + 0.5 * preact * (1.0 - tanh_value * tanh_value) * 0.7978845608 * (1.0 + 3.0 * 0.044715 * preact * preact)
    return activated, slopes


def reference(inputs, weight, cotangent):
    tokens_all = inputs.shape[0]
    width = inputs.shape[1]
    hidden = weight.shape[1]
    feat_block = width // N_COL
    unit_block = hidden // N_ROW
    input_blocks = inputs.reshape(tokens_all, N_COL, feat_block).transpose(1, 0, 2)
    weight_blocks = weight.reshape(N_COL, feat_block, hidden)

    def forward_step(total, pieces):
        term = jnp.dot(pieces[0], pieces[1], preferred_element_type=jnp.float32)
        return total + term.astype(jnp.bfloat16).astype(jnp.float32), None

    preact, _ = lax.scan(forward_step, jnp.zeros((tokens_all, hidden), jnp.float32), (input_blocks, weight_blocks))
    activated, slopes = gelu_parts(preact)
    hidden_grad = (cotangent.astype(jnp.float32) * slopes).astype(jnp.bfloat16)
    grad_blocks = hidden_grad.reshape(tokens_all, N_ROW, unit_block).transpose(1, 0, 2)
    column_blocks = weight.reshape(width, N_ROW, unit_block).transpose(1, 0, 2)

    def backward_step(total, pieces):
        term = lax.dot_general(pieces[0], pieces[1], (((1,), (1,)), ((), ())), preferred_element_type=jnp.float32)
        return total + term.astype(jnp.bfloat16).astype(jnp.float32), None

    grad_total, _ = lax.scan(backward_step, jnp.zeros((tokens_all, width), jnp.float32), (grad_blocks, column_blocks))
    grad_inputs = grad_total.astype(jnp.bfloat16)
    grad_weight = jnp.dot(inputs.T, hidden_grad, preferred_element_type=jnp.float32).astype(jnp.bfloat16)
    return activated.astype(jnp.bfloat16), grad_inputs, grad_weight
```

```python
import jax
import jax.numpy as jnp
from jax import lax
from jax.sharding import Mesh
from jax.sharding import PartitionSpec as P

Z, X, Y, C = 8, 4, 8, 2


def gelu_parts(preact):
    tanh_arg = 0.7978845608 * (preact + 0.044715 * preact * preact * preact)
    tanh_value = jnp.tanh(tanh_arg)
    activated = 0.5 * preact * (1.0 + tanh_value)
    slopes = 0.5 * (1.0 + tanh_value) + 0.5 * preact * (
        1.0 - tanh_value * tanh_value
    ) * 0.7978845608 * (1.0 + 3.0 * 0.044715 * preact * preact)
    return (activated, slopes)


def exchange(x, axis):
    return lax.all_to_all(x, axis, 0, 0, tiled=True)


def spread(x, axis, n):
    return exchange(jnp.broadcast_to(x[None], (n, *x.shape)), axis)


def swap_cores(x):
    return lax.ppermute(x, "c", [(0, 1), (1, 0)])


def total(x):
    return jnp.sum(x.astype(jnp.float32), axis=0)


def body(inputs, weight, cotangent):
    core = lax.axis_index("c")
    tokens, width = inputs.shape
    rows, hidden = cotangent.shape

    by_z = spread(inputs, "z", Z)
    by_x = spread(by_z.reshape(Z * tokens, width), "x", X)
    gathered = by_x.reshape(X, Z, tokens, width).transpose(1, 0, 2, 3).reshape(-1, width)

    partial = jnp.dot(gathered, weight, preferred_element_type=jnp.float32)
    partial = partial.astype(jnp.bfloat16).reshape(Y, C, rows, hidden)
    mine = lax.dynamic_index_in_dim(partial, core, 1, keepdims=False)
    theirs = lax.dynamic_index_in_dim(partial, 1 - core, 1, keepdims=False)
    pair = (mine.astype(jnp.float32) + swap_cores(theirs).astype(jnp.float32)).astype(jnp.bfloat16)
    preact = total(exchange(pair, "y"))

    gelu_local, slopes = gelu_parts(preact)
    activated = gelu_local.astype(jnp.bfloat16)
    local_grad = (cotangent.astype(jnp.float32) * slopes).astype(jnp.bfloat16)

    mine = spread(local_grad, "y", Y)
    theirs = swap_cores(mine)
    first = jnp.where(core == 0, mine, theirs)
    second = jnp.where(core == 0, theirs, mine)
    hidden_grad = jnp.stack([first, second], axis=1).reshape(-1, hidden)

    partial = lax.dot_general(
        hidden_grad, weight, (((1,), (1,)), ((), ())), preferred_element_type=jnp.float32
    ).astype(jnp.bfloat16)
    partial = partial.reshape(Z, X, tokens, width).transpose(1, 0, 2, 3)
    sums = total(exchange(partial, "x")).astype(jnp.bfloat16)
    grad_inputs = total(exchange(sums, "z")).astype(jnp.bfloat16)

    grad_weight = lax.dot_general(
        gathered, hidden_grad, (((0,), (0,)), ((), ())), preferred_element_type=jnp.float32
    ).astype(jnp.bfloat16)
    return (activated, grad_inputs, grad_weight)


def solution(mesh):
    grid = Mesh(mesh.devices.reshape(Z, X, Y, C), ("z", "x", "y", "c"))
    row, col = ("z", "x"), ("y", "c")
    return jax.shard_map(
        body,
        mesh=grid,
        in_specs=(P(row, col), P(col, row), P(col, row)),
        out_specs=(P(col, row), P(row, col), P(col, row)),
        check_vma=False,
    )
```

```python
import jax
import jax.numpy as jnp
from jax import lax
from jax.sharding import Mesh
from jax.sharding import PartitionSpec as P

Z, X, Y, C = 8, 4, 8, 2
ALL = ("z", "x", "y", "c")


def gelu_parts(preact):
    tanh_arg = 0.7978845608 * (preact + 0.044715 * preact * preact * preact)
    tanh_value = jnp.tanh(tanh_arg)
    activated = 0.5 * preact * (1.0 + tanh_value)
    slopes = 0.5 * (1.0 + tanh_value) + 0.5 * preact * (
        1.0 - tanh_value * tanh_value
    ) * 0.7978845608 * (1.0 + 3.0 * 0.044715 * preact * preact)
    return (activated, slopes)


def z_groups():
    groups = []
    for x in range(X):
        for y in range(Y):
            for c in range(C):
                sign = 1 if c == 0 else -1
                groups.append([(((y + sign * j) % Z * X + x) * Y + y) * C + c for j in range(Z)])
    return groups


def exchange_z(x):
    return lax.all_to_all(x, ALL, 0, 0, tiled=True, axis_index_groups=z_groups())


def exchange_x(x):
    return lax.all_to_all(x, "x", 0, 0, tiled=True)


def copies(x, n):
    return jnp.broadcast_to(x[None], (n, *x.shape))


def swap_cores(x):
    return lax.ppermute(x, "c", [(0, 1), (1, 0)])


def send(x, distance):
    pairs = []
    for y in range(Y):
        pairs.append((y * C, (y + distance) % Y * C))
        pairs.append((y * C + 1, (y - distance) % Y * C + 1))
    return lax.ppermute(x, ("y", "c"), pairs)


def f32(x):
    return x.astype(jnp.float32)


def bf16(x):
    return x.astype(jnp.bfloat16)


def total(x):
    return jnp.sum(f32(x), axis=0)


def body(inputs, weight, cotangent):
    core = lax.axis_index("c")
    first = core == 0
    tokens, width = inputs.shape
    rows, hidden = cotangent.shape
    half = hidden // 2
    block = X * tokens

    def half_of(x):
        return jnp.where(first, x[:, :half], x[:, half:])

    other = swap_cores(cotangent)
    cotangents = jnp.concatenate(
        [jnp.where(first, cotangent, other), jnp.where(first, other, cotangent)], axis=0
    )

    by_z = exchange_z(copies(inputs, Z))
    by_x = exchange_x(copies(by_z, X).reshape(X, Z, tokens, width))
    gathered = by_x.transpose(1, 0, 2, 3).reshape(Z, block, width)

    def product(lo, hi):
        out = jnp.dot(
            gathered[lo:hi].reshape(-1, width), weight, preferred_element_type=jnp.float32
        )
        return bf16(out).reshape(hi - lo, block, hidden)

    far = product(4, 6)
    far_other = swap_cores(far)
    near = product(6, 8)
    near_other = swap_cores(near)
    mine = product(0, 4)

    four = bf16(half_of(f32(far[0]) + f32(far_other[0])))
    three = bf16(f32(mine[3]) + f32(far_other[1]))
    four = send(four, 2)
    three = send(three, 1)
    one = send(bf16(f32(mine[1]) + f32(near_other[1])), 1)
    two = f32(mine[2]) + f32(near_other[0]) + f32(three)
    zero = jnp.zeros_like(four)
    four = jnp.concatenate(
        [jnp.where(first, four, zero), jnp.where(first, zero, four)], axis=1
    )
    two = send(bf16(two + f32(four)), 2)
    partial = f32(mine[0]) + f32(one) + f32(two)
    preact = partial + f32(swap_cores(bf16(partial)))

    gelu_local, slopes = gelu_parts(preact)
    activated = bf16(jnp.where(first, gelu_local[:rows], gelu_local[rows:]))
    own = bf16(f32(cotangents) * slopes)

    two = send(own, 2)
    one = send(own, 1)
    three = send(two, 1)
    four = send(half_of(two), 2)
    four_other = swap_cores(four)
    four = jnp.concatenate(
        [jnp.where(first, four, four_other), jnp.where(first, four_other, four)], axis=1
    )
    hidden_grad = jnp.concatenate(
        [own, swap_cores(one), swap_cores(two), swap_cores(three), four, three, two, one], axis=0
    )

    partial = bf16(
        lax.dot_general(
            hidden_grad, weight, (((1,), (1,)), ((), ())), preferred_element_type=jnp.float32
        )
    )
    partial = partial.reshape(Z, X, tokens, width).transpose(1, 0, 2, 3)
    sums = bf16(total(exchange_x(partial)))
    grad_inputs = bf16(total(exchange_z(sums)))

    grad_weight = bf16(
        lax.dot_general(
            gathered.reshape(-1, width),
            hidden_grad,
            (((0,), (0,)), ((), ())),
            preferred_element_type=jnp.float32,
        )
    )
    return (activated, grad_inputs, grad_weight)


def solution(mesh):
    grid = Mesh(mesh.devices.reshape(Z, X, Y, C), ALL)
    row, col = ("z", "x"), ("y", "c")
    return jax.shard_map(
        body,
        mesh=grid,
        in_specs=(P(row, col), P(col, row), P(col, row)),
        out_specs=(P(col, row), P(row, col), P(col, row)),
        check_vma=False,
    )
```

```python
import jax
import jax.numpy as jnp
from jax import lax
from jax.experimental import pallas as pl
from jax.experimental.pallas import tpu as pltpu
from jax.sharding import Mesh
from jax.sharding import PartitionSpec as P

Z, X, Y, C = 8, 4, 8, 2
ALL = ("z", "x", "y", "c")


def gelu_parts(preact):
    tanh_arg = 0.7978845608 * (preact + 0.044715 * preact * preact * preact)
    tanh_value = jnp.tanh(tanh_arg)
    activated = 0.5 * preact * (1.0 + tanh_value)
    slopes = 0.5 * (1.0 + tanh_value) + 0.5 * preact * (
        1.0 - tanh_value * tanh_value
    ) * 0.7978845608 * (1.0 + 3.0 * 0.044715 * preact * preact)
    return (activated, slopes)


def z_groups():
    groups = []
    for x in range(X):
        for y in range(Y):
            for c in range(C):
                sign = 1 if c == 0 else -1
                groups.append([(((y + sign * j) % Z * X + x) * Y + y) * C + c for j in range(Z)])
    return groups


def exchange_z(x):
    return lax.all_to_all(x, ALL, 0, 0, tiled=True, axis_index_groups=z_groups())


def exchange_x(x):
    return lax.all_to_all(x, "x", 0, 0, tiled=True)


def copies(x, n):
    return jnp.broadcast_to(x[None], (n, *x.shape))


def swap_cores(x):
    return lax.ppermute(x, "c", [(0, 1), (1, 0)])


def send(x, distance):
    pairs = []
    for y in range(Y):
        pairs.append((y * C, (y + distance) % Y * C))
        pairs.append((y * C + 1, (y - distance) % Y * C + 1))
    return lax.ppermute(x, ("y", "c"), pairs)


def f32(x):
    return x.astype(jnp.float32)


def bf16(x):
    return x.astype(jnp.bfloat16)


def total(x):
    return jnp.sum(f32(x), axis=0)


def outer(x, y, columns=256):
    def kernel(x_ref, y_ref, out_ref):
        out_ref[...] = lax.dot_general(
            x_ref[...], y_ref[...], (((0,), (0,)), ((), ())), preferred_element_type=jnp.float32
        ).astype(out_ref.dtype)

    (rows, left), right = x.shape, y.shape[1]
    return pl.pallas_call(
        kernel,
        grid=(right // columns,),
        in_specs=[
            pl.BlockSpec((rows, left), lambda i: (0, 0)),
            pl.BlockSpec((rows, columns), lambda i: (0, i)),
        ],
        out_specs=pl.BlockSpec((left, columns), lambda i: (0, i)),
        out_shape=jax.ShapeDtypeStruct((left, right), x.dtype),
        compiler_params=pltpu.CompilerParams(vmem_limit_bytes=16 * 2**20),
        cost_estimate=pl.CostEstimate(
            flops=2 * rows * left * right,
            bytes_accessed=2 * (rows * left + rows * right + left * right),
            transcendentals=0,
        ),
    )(x, y)


def body(inputs, weight, cotangent):
    core = lax.axis_index("c")
    first = core == 0
    tokens, width = inputs.shape
    rows, hidden = cotangent.shape
    half = hidden // 2
    block = X * tokens

    def half_of(x):
        return jnp.where(first, x[:, :half], x[:, half:])

    other = swap_cores(cotangent)
    cotangents = jnp.concatenate(
        [jnp.where(first, cotangent, other), jnp.where(first, other, cotangent)], axis=0
    )

    by_z = exchange_z(copies(inputs, Z))
    by_x = exchange_x(copies(by_z, X).reshape(X, Z, tokens, width))
    by_x, cotangents = lax.optimization_barrier((by_x, cotangents))
    gathered = by_x.transpose(1, 0, 2, 3).reshape(Z, block, width)

    def product(x):
        out = jnp.dot(x.reshape(-1, width), weight, preferred_element_type=jnp.float32)
        return bf16(out).reshape(-1, block, hidden)

    lent = product(gathered[4:8])
    theirs = swap_cores(lent)
    mine = product(gathered[0:4])
    four = send(bf16(half_of(f32(lent[0]) + f32(theirs[0]))), 2)
    ahead = [bf16(f32(mine[3]) + f32(theirs[1])), bf16(f32(mine[1]) + f32(theirs[3]))]
    ahead = send(jnp.concatenate(ahead, axis=0), 1)
    three, one = ahead[:block], ahead[block:]
    two = f32(mine[2]) + f32(theirs[2]) + f32(three)
    zero = jnp.zeros_like(four)
    four = jnp.concatenate(
        [jnp.where(first, four, zero), jnp.where(first, zero, four)], axis=1
    )
    two = send(bf16(two + f32(four)), 2)
    partial = f32(mine[0]) + f32(one) + f32(two)
    preact = partial + f32(swap_cores(bf16(partial)))

    gelu_local, slopes = gelu_parts(preact)
    activated = bf16(jnp.where(first, gelu_local[:rows], gelu_local[rows:]))
    own = bf16(f32(cotangents) * slopes)

    two = send(own, 2)
    one = send(own, 1)
    three = send(two, 1)
    four = half_of(two)
    early, four, activated = lax.optimization_barrier(
        (jnp.concatenate([one, two], axis=0), four, activated)
    )
    four = send(four, 2)
    early = swap_cores(early)
    late = swap_cores(jnp.concatenate([three, four], axis=1))
    four_other = late[:, hidden:]
    four = jnp.concatenate(
        [jnp.where(first, four, four_other), jnp.where(first, four_other, four)], axis=1
    )
    hidden_grad = jnp.concatenate(
        [own, early, late[:, :hidden], four, three, two, one], axis=0
    )

    partial = bf16(
        lax.dot_general(
            hidden_grad, weight, (((1,), (1,)), ((), ())), preferred_element_type=jnp.float32
        )
    )
    partial = partial.reshape(Z, X, tokens, width).transpose(1, 0, 2, 3)
    grad_weight = outer(gathered.reshape(-1, width), hidden_grad)
    sums = bf16(total(exchange_x(partial)))
    grad_inputs = bf16(total(exchange_z(sums)))
    return (activated, grad_inputs, grad_weight)


def solution(mesh):
    grid = Mesh(mesh.devices.reshape(Z, X, Y, C), ALL)
    row, col = ("z", "x"), ("y", "c")
    return jax.shard_map(
        body,
        mesh=grid,
        in_specs=(P(row, col), P(col, row), P(col, row)),
        out_specs=(P(col, row), P(row, col), P(col, row)),
        check_vma=False,
    )
```

```python
import jax
import jax.numpy as jnp
from jax import lax
from jax.sharding import Mesh
from jax.sharding import PartitionSpec as P

Z, X, Y, C = 8, 4, 8, 2
ALL = ("z", "x", "y", "c")


def gelu_parts(preact):
    tanh_arg = 0.7978845608 * (preact + 0.044715 * preact * preact * preact)
    tanh_value = jnp.tanh(tanh_arg)
    activated = 0.5 * preact * (1.0 + tanh_value)
    slopes = 0.5 * (1.0 + tanh_value) + 0.5 * preact * (
        1.0 - tanh_value * tanh_value
    ) * 0.7978845608 * (1.0 + 3.0 * 0.044715 * preact * preact)
    return (activated, slopes)


def z_groups():
    groups = []
    for x in range(X):
        for y in range(Y):
            for c in range(C):
                sign = 1 if c == 0 else -1
                groups.append([(((y + sign * j) % Z * X + x) * Y + y) * C + c for j in range(Z)])
    return groups


def exchange_z(x):
    return lax.all_to_all(x, ALL, 0, 0, tiled=True, axis_index_groups=z_groups())


def exchange_x(x):
    return lax.all_to_all(x, "x", 0, 0, tiled=True)


def copies(x, n):
    return jnp.broadcast_to(x[None], (n, *x.shape))


def swap_cores(x):
    return lax.ppermute(x, "c", [(0, 1), (1, 0)])


def send(x, distance):
    pairs = []
    for y in range(Y):
        pairs.append((y * C, (y + distance) % Y * C))
        pairs.append((y * C + 1, (y - distance) % Y * C + 1))
    return lax.ppermute(x, ("y", "c"), pairs)


def f32(x):
    return x.astype(jnp.float32)


def bf16(x):
    return x.astype(jnp.bfloat16)


def total(x):
    return jnp.sum(f32(x), axis=0)


def body(inputs, weight, cotangent):
    first = lax.axis_index("c") == 0
    inputs, first = lax.optimization_barrier((inputs, first))
    tokens, width = inputs.shape
    rows, hidden = cotangent.shape
    half = hidden // 2
    block = X * tokens

    def half_of(x):
        return jnp.where(first, x[:, :half], x[:, half:])

    other = swap_cores(cotangent)
    cotangents = jnp.concatenate(
        [jnp.where(first, cotangent, other), jnp.where(first, other, cotangent)], axis=0
    )

    by_z = exchange_z(copies(inputs, Z))
    by_x = lax.all_gather(by_z[1:].reshape(-1, width), "x", axis=0, tiled=True)
    by_x = by_x.reshape(X, Z - 1, tokens, width).transpose(1, 0, 2, 3)
    gathered = by_x.reshape(Z - 1, block, width)
    own_x = exchange_x(copies(by_z[0], X)).reshape(1, block, width)

    def product(x):
        out = jnp.dot(x.reshape(-1, width), weight, preferred_element_type=jnp.float32)
        return bf16(out).reshape(-1, block, hidden)

    lent = product(gathered[3:7])
    theirs = swap_cores(lent)
    mine = product(gathered[0:3])
    four = send(bf16(half_of(f32(lent[0]) + f32(theirs[0]))), 2)
    ahead = [bf16(f32(mine[2]) + f32(theirs[1])), bf16(f32(mine[0]) + f32(theirs[3]))]
    ahead = send(jnp.concatenate(ahead, axis=0), 1)
    three, one = ahead[:block], ahead[block:]
    four, own_x = lax.optimization_barrier((four, own_x))
    two = f32(mine[1]) + f32(theirs[2]) + f32(three)
    zero = jnp.zeros_like(four)
    four = jnp.concatenate(
        [jnp.where(first, four, zero), jnp.where(first, zero, four)], axis=1
    )
    two = send(bf16(two + f32(four)), 2)
    partial = f32(product(own_x)[0]) + f32(one) + f32(two)
    preact = partial + f32(swap_cores(bf16(partial)))

    gelu_local, slopes = gelu_parts(preact)
    activated = bf16(jnp.where(first, gelu_local[:rows], gelu_local[rows:]))
    own = bf16(f32(cotangents) * slopes)

    two = send(own, 2)
    one = send(own, 1)
    three = send(two, 1)
    four = half_of(two)
    turned = jnp.concatenate([own_x, gathered], axis=0).reshape(-1, width).T
    early, four, activated, turned = lax.optimization_barrier(
        (jnp.concatenate([one, two], axis=0), four, activated, turned)
    )
    four = send(four, 2)
    early = swap_cores(early)
    late = swap_cores(jnp.concatenate([three, four], axis=1))
    four_other = late[:, hidden:]
    four = jnp.concatenate(
        [jnp.where(first, four, four_other), jnp.where(first, four_other, four)], axis=1
    )
    hidden_grad = jnp.concatenate(
        [own, early, late[:, :hidden], four, three, two, one], axis=0
    )

    partial = bf16(
        lax.dot_general(
            hidden_grad, weight, (((1,), (1,)), ((), ())), preferred_element_type=jnp.float32
        )
    )
    partial = partial.reshape(Z, X, tokens, width).transpose(1, 0, 2, 3)
    sums = bf16(total(exchange_x(partial)))
    grad_inputs = bf16(total(exchange_z(sums)))
    grad_weight = bf16(jnp.dot(turned, hidden_grad, preferred_element_type=jnp.float32))
    return (activated, grad_inputs, grad_weight)


def solution(mesh):
    grid = Mesh(mesh.devices.reshape(Z, X, Y, C), ALL)
    row, col = ("z", "x"), ("y", "c")
    return jax.shard_map(
        body,
        mesh=grid,
        in_specs=(P(row, col), P(col, row), P(col, row)),
        out_specs=(P(col, row), P(row, col), P(col, row)),
        check_vma=False,
    )
```

```python
import jax
import jax.numpy as jnp
from jax import lax
from jax.sharding import Mesh
from jax.sharding import PartitionSpec as P

Z, X, Y, C = 8, 4, 8, 2
ALL = ("z", "x", "y", "c")


def gelu_parts(preact):
    tanh_arg = 0.7978845608 * (preact + 0.044715 * preact * preact * preact)
    tanh_value = jnp.tanh(tanh_arg)
    activated = 0.5 * preact * (1.0 + tanh_value)
    slopes = 0.5 * (1.0 + tanh_value) + 0.5 * preact * (
        1.0 - tanh_value * tanh_value
    ) * 0.7978845608 * (1.0 + 3.0 * 0.044715 * preact * preact)
    return (activated, slopes)


def z_groups():
    groups = []
    for x in range(X):
        for y in range(Y):
            for c in range(C):
                sign = 1 if c == 0 else -1
                groups.append([(((y + sign * j) % Z * X + x) * Y + y) * C + c for j in range(Z)])
    return groups


def exchange_z(x):
    return lax.all_to_all(x, ALL, 0, 0, tiled=True, axis_index_groups=z_groups())


def exchange_x(x):
    return lax.all_to_all(x, "x", 0, 0, tiled=True)


def copies(x, n):
    return jnp.broadcast_to(x[None], (n, *x.shape))


def swap_cores(x):
    return lax.ppermute(x, "c", [(0, 1), (1, 0)])


def send(x, distance):
    pairs = []
    for y in range(Y):
        pairs.append((y * C, (y + distance) % Y * C))
        pairs.append((y * C + 1, (y - distance) % Y * C + 1))
    return lax.ppermute(x, ("y", "c"), pairs)


def f32(x):
    return x.astype(jnp.float32)


def bf16(x):
    return x.astype(jnp.bfloat16)


def total(x):
    return jnp.sum(f32(x), axis=0)


def body(inputs, weight, cotangent):
    first = lax.axis_index("c") == 0
    inputs, first = lax.optimization_barrier((inputs, first))
    tokens, width = inputs.shape
    rows, hidden = cotangent.shape
    half = hidden // 2
    block = X * tokens

    def half_of(x):
        return jnp.where(first, x[:, :half], x[:, half:])

    by_z = exchange_z(copies(inputs, Z))
    by_x = lax.all_gather(by_z[1:].reshape(-1, width), "x", axis=0, tiled=True)
    by_x = by_x.reshape(X, Z - 1, tokens, width).transpose(1, 0, 2, 3)
    gathered = by_x.reshape(Z - 1, block, width)
    own_x = exchange_x(copies(by_z[0], X)).reshape(1, block, width)

    def product(x):
        out = jnp.dot(x.reshape(-1, width), weight, preferred_element_type=jnp.float32)
        return bf16(out).reshape(-1, block, hidden)

    lent = product(gathered[3:7])
    theirs = swap_cores(lent)
    mine = product(gathered[0:3])
    four = send(bf16(half_of(f32(lent[0]) + f32(theirs[0]))), 2)
    three = send(bf16(f32(mine[2]) + f32(theirs[1])), 1)
    one = send(bf16(f32(mine[0]) + f32(theirs[3])), 1)
    two = f32(mine[1]) + f32(theirs[2]) + f32(three)
    zero = jnp.zeros_like(four)
    four = jnp.concatenate(
        [jnp.where(first, four, zero), jnp.where(first, zero, four)], axis=1
    )
    two = send(bf16(two + f32(four)), 2)
    partial = f32(product(own_x)[0]) + f32(one) + f32(two)
    other = swap_cores(jnp.concatenate([bf16(partial), cotangent], axis=0))
    preact = partial + f32(other[:block])
    other = other[block:]
    cotangents = jnp.concatenate(
        [jnp.where(first, cotangent, other), jnp.where(first, other, cotangent)], axis=0
    )

    gelu_local, slopes = gelu_parts(preact)
    activated = bf16(jnp.where(first, gelu_local[:rows], gelu_local[rows:]))
    own = bf16(f32(cotangents) * slopes)

    two = send(own, 2)
    one = send(own, 1)
    three = send(two, 1)
    four = half_of(two)
    turned = jnp.concatenate([own_x, gathered], axis=0).reshape(-1, width).T
    early, four, activated, turned = lax.optimization_barrier(
        (jnp.concatenate([one, two], axis=0), four, activated, turned)
    )
    four = send(four, 2)
    early = swap_cores(early)
    late = swap_cores(jnp.concatenate([three, four], axis=1))
    four_other = late[:, hidden:]
    four = jnp.concatenate(
        [jnp.where(first, four, four_other), jnp.where(first, four_other, four)], axis=1
    )
    hidden_grad = jnp.concatenate(
        [own, early, late[:, :hidden], four, three, two, one], axis=0
    )

    partial = bf16(
        lax.dot_general(
            hidden_grad, weight, (((1,), (1,)), ((), ())), preferred_element_type=jnp.float32
        )
    )
    partial = partial.reshape(Z, X, tokens, width).transpose(1, 0, 2, 3)
    sums = bf16(total(exchange_x(partial)))
    grad_inputs = bf16(total(exchange_z(sums)))
    grad_weight = bf16(jnp.dot(turned, hidden_grad, preferred_element_type=jnp.float32))
    return (activated, grad_inputs, grad_weight)


def solution(mesh):
    grid = Mesh(mesh.devices.reshape(Z, X, Y, C), ALL)
    row, col = ("z", "x"), ("y", "c")
    return jax.shard_map(
        body,
        mesh=grid,
        in_specs=(P(row, col), P(col, row), P(col, row)),
        out_specs=(P(col, row), P(row, col), P(col, row)),
        check_vma=False,
    )
```

```python
import jax
import jax.numpy as jnp
from jax import lax
from jax.sharding import Mesh
from jax.sharding import PartitionSpec as P

Z, X, Y, C = 8, 4, 8, 2
ALL = ("z", "x", "y", "c")


def gelu_parts(preact):
    tanh_arg = 0.7978845608 * (preact + 0.044715 * preact * preact * preact)
    tanh_value = jnp.tanh(tanh_arg)
    activated = 0.5 * preact * (1.0 + tanh_value)
    slopes = 0.5 * (1.0 + tanh_value) + 0.5 * preact * (
        1.0 - tanh_value * tanh_value
    ) * 0.7978845608 * (1.0 + 3.0 * 0.044715 * preact * preact)
    return (activated, slopes)


def z_groups():
    groups = []
    for x in range(X):
        for y in range(Y):
            for c in range(C):
                sign = 1 if c == 0 else -1
                groups.append([(((y + sign * j) % Z * X + x) * Y + y) * C + c for j in range(Z)])
    return groups


def exchange_z(x):
    return lax.all_to_all(x, ALL, 0, 0, tiled=True, axis_index_groups=z_groups())


def exchange_x(x):
    return lax.all_to_all(x, "x", 0, 0, tiled=True)


def copies(x, n):
    return jnp.broadcast_to(x[None], (n, *x.shape))


def swap_cores(x):
    return lax.ppermute(x, "c", [(0, 1), (1, 0)])


def send(x, distance):
    pairs = []
    for y in range(Y):
        pairs.append((y * C, (y + distance) % Y * C))
        pairs.append((y * C + 1, (y - distance) % Y * C + 1))
    return lax.ppermute(x, ("y", "c"), pairs)


def f32(x):
    return x.astype(jnp.float32)


def bf16(x):
    return x.astype(jnp.bfloat16)


def total(x):
    return jnp.sum(f32(x), axis=0)


def body(inputs, weight, cotangent):
    first = lax.axis_index("c") == 0
    inputs, first = lax.optimization_barrier((inputs, first))
    tokens, width = inputs.shape
    rows, hidden = cotangent.shape
    half = hidden // 2
    block = X * tokens

    def half_of(x):
        return jnp.where(first, x[:, :half], x[:, half:])

    by_z = exchange_z(copies(inputs, Z))
    by_x = lax.all_gather(by_z[1:].reshape(-1, width), "x", axis=0, tiled=True)
    by_x = by_x.reshape(X, Z - 1, tokens, width).transpose(1, 0, 2, 3)
    gathered = by_x.reshape(Z - 1, block, width)
    own_x = exchange_x(copies(by_z[0], X)).reshape(1, block, width)

    def product(x):
        out = jnp.dot(x.reshape(-1, width), weight, preferred_element_type=jnp.float32)
        return bf16(out).reshape(-1, block, hidden)

    lent = product(gathered[3:7])
    theirs = swap_cores(lent)
    mine = product(gathered[0:3])
    four = send(bf16(half_of(f32(lent[0]) + f32(theirs[0]))), 2)
    three = send(bf16(f32(mine[2]) + f32(theirs[1])), 1)
    one = send(bf16(f32(mine[0]) + f32(theirs[3])), 1)
    two = f32(mine[1]) + f32(theirs[2]) + f32(three)
    zero = jnp.zeros_like(four)
    four = jnp.concatenate(
        [jnp.where(first, four, zero), jnp.where(first, zero, four)], axis=1
    )
    two = send(bf16(two + f32(four)), 2)
    partial = f32(product(own_x)[0]) + f32(one) + f32(two)
    other = swap_cores(jnp.concatenate([bf16(partial), cotangent], axis=0))
    preact = partial + f32(other[:block])
    other, gathered = lax.optimization_barrier((other[block:], gathered))
    cotangents = jnp.concatenate(
        [jnp.where(first, cotangent, other), jnp.where(first, other, cotangent)], axis=0
    )

    gelu_local, slopes = gelu_parts(preact)
    activated = bf16(jnp.where(first, gelu_local[:rows], gelu_local[rows:]))
    own = bf16(f32(cotangents) * slopes)

    two = send(own, 2)
    one = send(own, 1)
    three = send(two, 1)
    four = half_of(two)
    turned = jnp.concatenate([own_x, gathered], axis=0).reshape(-1, width).T
    early, four, activated, turned = lax.optimization_barrier(
        (jnp.concatenate([one, two], axis=0), four, activated, turned)
    )
    four = send(four, 2)
    early = swap_cores(early)
    late = swap_cores(jnp.concatenate([three, four], axis=1))
    four_other = late[:, hidden:]
    four = jnp.concatenate(
        [jnp.where(first, four, four_other), jnp.where(first, four_other, four)], axis=1
    )
    hidden_grad = jnp.concatenate(
        [own, early, late[:, :hidden], four, three, two, one], axis=0
    )

    partial = bf16(
        lax.dot_general(
            hidden_grad, weight, (((1,), (1,)), ((), ())), preferred_element_type=jnp.float32
        )
    )
    partial = partial.reshape(Z, X, tokens, width).transpose(1, 0, 2, 3)
    sums = bf16(total(exchange_x(partial)))
    grad_inputs = bf16(total(exchange_z(sums)))
    grad_weight = bf16(jnp.dot(turned, hidden_grad, preferred_element_type=jnp.float32))
    return (activated, grad_inputs, grad_weight)


def solution(mesh):
    grid = Mesh(mesh.devices.reshape(Z, X, Y, C), ALL)
    row, col = ("z", "x"), ("y", "c")
    return jax.shard_map(
        body,
        mesh=grid,
        in_specs=(P(row, col), P(col, row), P(col, row)),
        out_specs=(P(col, row), P(row, col), P(col, row)),
        check_vma=False,
    )
```
